32 devices in a mesh: dp: 8 (over y, x, core), expert: 4 (over z).
Axes of the slice: x: 2, y: 2, z: 4, core: 2. Of those that a mesh axis runs over, the one named last changes fastest.
Arguments:
- residual: bfloat16 [512, 4096], P('dp', 'expert'), may hold values from -6 to 6
- queries: bfloat16 [512, 4096], P('dp', 'expert'), may hold values from -25 to 25
- cache_keys: bfloat16 [18432, 1024], P('dp', 'expert'), may hold values from -5 to 5
- cache_values: bfloat16 [18432, 1024], P('dp', 'expert'), may hold values from -18 to 18
- node_of_position: int32 [18432], P('dp'), may hold values from -1 to 20, as said below
- parent: int32 [21], replicated, may hold values from 0 to 4, as said below
- leaf_ids: int32 [512], P('dp'), may hold values from 5 to 20
- routes: int32 [512, 2], P('dp'), may hold values from 0 to 7, all different within a row; in each aligned block of 64 rows (0 to 63, 64 to 127, ...) at most 32 rows name the same one
- gate_weights: bfloat16 [512, 2], P('dp'), may hold values from 0.19921875 to 0.796875
- norm_gain: bfloat16 [4096], replicated, may hold values from 0.5 to 1.5
- w_gate: bfloat16 [8, 4096, 14336], P('expert', None, 'dp'), may hold values from -0.09375 to 0.09375
- w_up: bfloat16 [8, 4096, 14336], P('expert', None, 'dp'), may hold values from -0.09375 to 0.09375
- w_down: bfloat16 [8, 14336, 4096], P('expert', 'dp'), may hold values from -0.046875 to 0.046875
Outputs:
- attention_out: bfloat16 [512, 4096], P('dp', 'expert')
- layer_out: bfloat16 [512, 4096], P('dp', 'expert')
The draws below stay inside these ranges and needn't reach their ends.
Inputs may be any that keep to these rules, and one draw needn't show every extreme that they name: `node_of_position`: each block of 2304 positions begins with 256 positions of node 0, the root; the rest come in blocks of 128 positions, each holding one non-root node on a leading run of one or more positions and -1 after it; every non-root node holds one or more blocks. Node 0 is the root and its own parent; nodes 1 to 4 have parent 0; the other nodes are leaves with a parent among nodes 1 to 4. `leaf_ids`: every request sits at a leaf. `routes`: the two experts of a request differ; among the 64 requests of one index of dp no expert is named more than 32 times.
All inputs are finite; a program needn't handle non-finite values.
Results may differ from the reference program's by a relative error of at most 0.012.
Values may be sent and summed in bfloat16 or wider, within the bound.
A program may use at most 192 MiB of HBM per device.

```python
import math
import jax
import jax.numpy as jnp
import numpy as np
from jax import lax

D = 4096
Q_HEADS = 32
KV_HEADS = 8
HEAD_DIM = 128
FF = 14336
EXPERTS = 8
ROWS_DP = 64
ROOT_DEV = 256
BLOCKS_DEV = 16
BLOCK = 128
MIDS = 4
TOKENS = 512
CACHE_DEV = 2304
CACHE = 18432
NODES = 21
CAP = 32
N_DP = 8


def draw_queries(key, part):
    base_key = jax.random.fold_in(key, 11)
    values = 2.0 * jax.random.truncated_normal(base_key, -4.0, 4.0, (TOKENS, D), jnp.float32)
    return values.astype(jnp.bfloat16)


def draw_cache_keys(key, part):
    base_key = jax.random.fold_in(key, 23)
    values = jax.random.truncated_normal(base_key, -5.0, 5.0, (CACHE, KV_HEADS * HEAD_DIM), jnp.float32)
    return values.astype(jnp.bfloat16)


def draw_node_of_position(key, part):
    device_count = CACHE // CACHE_DEV
    block_count = device_count * BLOCKS_DEV
    block_order = jax.random.permutation(jax.random.fold_in(key, 31), block_count)
    owner_node = 1 + block_order % (NODES - 1)
    used_len = jax.random.randint(jax.random.fold_in(key, 37), (block_count,), 1, BLOCK + 1)
    used_len = jnp.where(block_order == 0, BLOCK, used_len)
    used_len = jnp.where(block_order == 1, 1, used_len)
    local_pos = jnp.arange(CACHE_DEV)
    offset = local_pos - ROOT_DEV
    block_local = jnp.maximum(offset, 0) // BLOCK
    within = jnp.maximum(offset, 0) % BLOCK
    device_ids = jnp.arange(device_count)
    block_ids = device_ids[:, None] * BLOCKS_DEV + block_local[None, :]
    node_ids = jnp.where(within[None, :] < used_len[block_ids], owner_node[block_ids], -1)
    node_ids = jnp.where(offset[None, :] < 0, 0, node_ids)
    return node_ids.reshape(CACHE).astype(jnp.int32)


def draw_parent(key, part):
    node_ids = jnp.arange(NODES)
    chosen = 1 + jax.random.randint(jax.random.fold_in(key, 41), (NODES,), 0, MIDS)
    chosen = jnp.where(node_ids == MIDS + 1, MIDS, chosen)
    return jnp.where(node_ids <= MIDS, 0, chosen).astype(jnp.int32)


def touch_ends(values, own_key, smallest, largest):
    longest = values.shape.index(max(values.shape))
    spots = []
    for shift in (0, 1):
        where = [jax.random.randint(jax.random.fold_in(own_key, axis), (), 0, length) for axis, length in enumerate(values.shape)]
        where[longest] = (where[longest] + shift) % values.shape[longest]
        spots.append(tuple(where))
    return values.at[spots[0]].set(smallest).at[spots[1]].set(largest)


def level_of(key, dims, shards, low, largest):
    level = 1.0
    for dim, blocks in shards:
        heights = jax.random.uniform(jax.random.fold_in(jax.random.fold_in(key, 6), dim), (blocks,), jnp.float32, low / len(shards), largest / len(shards))
        level = level * jnp.repeat(jnp.exp(heights), dims[dim] // blocks).reshape((-1,) + (1,) * (len(dims) - 1 - dim))
    return level


def routed_block(rng, own, number, rows, amount, top, bound, slope):
    ranking = jax.random.permutation(rng, amount)
    heavy_load, usual = shares(amount, rows * top, bound, slope, True), shares(amount, rows * top, bound, slope, False)
    places = jnp.arange(amount)

    def named(tallies, offset_by):
        used = int((tallies > 0).sum())
        fixed = max(1, used // 4)
        shifted = fixed + (places - fixed + offset_by * (used - fixed)) % max(1, amount - fixed)
        return jnp.zeros((amount,), jnp.int32).at[ranking[jnp.where(places < fixed, places, shifted)]].set(jnp.asarray(tallies, jnp.int32))

    tallies = jnp.where(number % 4 == 0, named(heavy_load, number // 4), named(usual, number - number // 4 - 1))
    mixed = jax.random.permutation(jax.random.fold_in(own, 3), amount)
    giver, sink = mixed[0:amount // 2 * 2:2], mixed[1:amount // 2 * 2:2]
    room = jnp.minimum(tallies[giver] - 1, bound - tallies[sink]) // 2
    room = jnp.where((giver == ranking[0]) | (sink == ranking[0]) | (tallies[sink] == 0), 0, jnp.maximum(room, 0))
    shifted = jax.random.randint(jax.random.fold_in(own, 4), (amount // 2,), 0, 1 << 20) % (room + 1)
    tallies = tallies.at[giver].add(-shifted).at[sink].add(shifted)
    members = jnp.searchsorted(jnp.cumsum(tallies), jnp.arange(rows * top), side="right").astype(jnp.int32)
    listing = members.reshape(top, rows).T
    listing = listing[jax.random.permutation(jax.random.fold_in(own, 1), rows)]
    offset_by = jax.random.randint(jax.random.fold_in(own, 2), (rows, 1), 0, top)
    return jnp.take_along_axis(listing, (jnp.arange(top)[None, :] + offset_by) % top, axis=1)


def shares(number_of, total, most, lean, full):
    loads = [(1 << 20) // math.isqrt(rank ** lean) + 1 for rank in range(1, number_of + 1)]
    largest = most if full else min(most, max(-(-total // number_of), total * loads[0] // sum(loads)))
    least = 1 if total - largest >= number_of - 1 else 0
    holding, spare = [largest] + [least] * (number_of - 1), total - largest - least * (number_of - 1)
    while spare > 0:
        candidates = [i for i in range(1, number_of) if holding[i] < largest] or [i for i in range(1, number_of) if holding[i] < most]
        mass, left = sum([loads[i] for i in candidates]), spare
        for i in candidates:
            addition = min(most - holding[i], max(1, left * loads[i] // mass), spare)
            holding[i] = holding[i] + addition
            spare = spare - addition
    return np.array(holding)


def bell_draw(own_key, extent, width, reach, split=(), kind=jnp.bfloat16):
    level = level_of(own_key, extent, split, -0.22, 0.18) if split else 1.0
    entries = jax.random.normal(own_key, extent, jnp.float32) * width * level
    return jnp.minimum(jnp.maximum(entries, -reach), reach).astype(kind)


def setup_inputs(seed: int = 0) -> dict:
    seeds = jax.random.split(jax.random.key(seed), 14)
    residual = bell_draw(seeds[0], (TOKENS, D), 1.0, 6.0, ((0, 8), (1, 4)))
    queries = draw_queries(jax.random.fold_in(seeds[13], 71), 0)
    cache_keys = draw_cache_keys(jax.random.fold_in(seeds[13], 71), 0)
    cache_values = bell_draw(seeds[3], (CACHE, KV_HEADS * HEAD_DIM), 3.0, 18.0, ((0, 8), (1, 4)))
    node_of_position = draw_node_of_position(jax.random.fold_in(seeds[13], 71), 0)
    parent = draw_parent(jax.random.fold_in(seeds[13], 71), 0)
    leaf_ids = touch_ends(jax.random.randint(seeds[6], (TOKENS,), MIDS + 1, NODES), jax.random.fold_in(seeds[6], 1), MIDS + 1, NODES - 1).astype(jnp.int32)
    routes_keys = jax.random.split(jax.random.fold_in(seeds[7], 1), TOKENS // ROWS_DP)
    routes_turns = jax.random.permutation(jax.random.fold_in(seeds[7], 3), TOKENS // ROWS_DP)
    routes = jax.vmap(lambda own, number: routed_block(jax.random.fold_in(seeds[7], 2), own, number, ROWS_DP, EXPERTS, 2, CAP, 2))(routes_keys, routes_turns).reshape((TOKENS, 2))
    gate_weights = jnp.clip(0.19921875 + 0.59765625 * jax.random.uniform(seeds[8], (TOKENS, 2), jnp.float32) ** level_of(seeds[8], (TOKENS, 2), ((0, 8),), -0.2, 0.2), 0.19921875, 0.796875).astype(jnp.bfloat16)
    norm_gain = jnp.clip(1.0 + 0.1 * jax.random.normal(seeds[9], (D,), jnp.float32), 0.5, 1.5).astype(jnp.bfloat16)
    w_gate = bell_draw(seeds[10], (EXPERTS, D, FF), D ** -0.5, 0.09375, ((0, 4), (2, 8)))
    w_up = bell_draw(seeds[11], (EXPERTS, D, FF), D ** -0.5, 0.09375, ((0, 4), (2, 8)))
    w_down = bell_draw(seeds[12], (EXPERTS, FF, D), FF ** -0.5, 0.046875, ((0, 4), (1, 8)))
    return dict(residual=residual, queries=queries, cache_keys=cache_keys, cache_values=cache_values, node_of_position=node_of_position, parent=parent, leaf_ids=leaf_ids, routes=routes, gate_weights=gate_weights, norm_gain=norm_gain, w_gate=w_gate, w_up=w_up, w_down=w_down)


def reference(residual, queries, cache_keys, cache_values, node_of_position, parent, leaf_ids, routes, gate_weights, norm_gain, w_gate, w_up, w_down):
    group_size = Q_HEADS // KV_HEADS
    score_scale = 1.0 / math.sqrt(HEAD_DIM)
    middle = parent[leaf_ids]
    upper = parent[middle]
    ancestors = jnp.stack([leaf_ids, middle, upper], axis=1)
    query_heads = queries.astype(jnp.float32).reshape(TOKENS, KV_HEADS, group_size, HEAD_DIM)
    key_blocks = cache_keys.reshape(N_DP, CACHE_DEV, KV_HEADS, HEAD_DIM)
    value_blocks = cache_values.reshape(N_DP, CACHE_DEV, KV_HEADS, HEAD_DIM)
    node_blocks = node_of_position.reshape(N_DP, CACHE_DEV)

    def one_owner(packed):
        keys_here, values_here, nodes_here = packed
        visible = jnp.any(nodes_here[None, :, None] == ancestors[:, None, :], axis=2)
        scores = jnp.einsum('tkgd,pkd->tkgp', query_heads, keys_here.astype(jnp.float32)) * score_scale
        scores = jnp.where(visible[:, None, None, :], scores, -jnp.inf)
        local_max = lax.optimization_barrier(jnp.max(scores, axis=3))
        exponent = jnp.exp(scores - local_max[..., None])
        local_total = lax.optimization_barrier(jnp.sum(exponent, axis=3))
        probs = exponent.astype(jnp.bfloat16)
        local_out = jnp.einsum('tkgp,pkd->tkgd', probs.astype(jnp.float32), values_here.astype(jnp.float32))
        return (local_max, local_total, local_out)
    maxima, totals, outputs = lax.map(one_owner, (key_blocks, value_blocks, node_blocks))
    global_max = lax.optimization_barrier(jnp.max(maxima, axis=0))
    factor = jnp.exp(maxima - global_max[None])
    attention = lax.optimization_barrier(jnp.sum(factor[..., None] * outputs, axis=0)) / lax.optimization_barrier(jnp.sum(factor * totals, axis=0))[..., None]
    attention = attention.reshape(TOKENS, D)
    attention_out = attention.astype(jnp.bfloat16)
    stream = (residual.astype(jnp.float32) + attention).astype(jnp.bfloat16)
    stream_wide = stream.astype(jnp.float32)
    inverse = lax.rsqrt(lax.optimization_barrier(jnp.mean(stream_wide * stream_wide, axis=1, keepdims=True)) + 1e-05)
    normed = (stream_wide * inverse * norm_gain.astype(jnp.float32)[None, :]).astype(jnp.bfloat16)
    flat_routes = routes.reshape(N_DP, ROWS_DP * 2)
    expert_hot = (flat_routes[:, :, None] == jnp.arange(EXPERTS, dtype=jnp.int32)[None, None, :]).astype(jnp.int32)
    slot_ranks = jnp.cumsum(expert_hot, axis=1) - expert_hot
    slot_ids = lax.optimization_barrier(jnp.sum(slot_ranks * expert_hot, axis=2)).reshape(-1)
    owner_rows = jnp.repeat(jnp.arange(N_DP, dtype=jnp.int32), ROWS_DP * 2)
    pair_tokens = jnp.repeat(jnp.arange(TOKENS, dtype=jnp.int32), 2)
    slot_index = (owner_rows * CAP + slot_ids).astype(jnp.int32)
    route_flat = flat_routes.reshape(-1)
    slot_table = jnp.full((EXPERTS, N_DP * CAP), TOKENS, dtype=jnp.int32)
    slot_table = slot_table.at[route_flat, slot_index].set(pair_tokens)
    normed_pad = jnp.concatenate([normed, jnp.zeros((1, D), jnp.bfloat16)], axis=0)

    def one_expert(packed):
        gate_mat, up_mat, down_mat, table_row = packed
        rows_in = jnp.take(normed_pad, table_row, axis=0)
        gate_val = jnp.dot(rows_in, gate_mat, preferred_element_type=jnp.float32)
        up_val = jnp.dot(rows_in, up_mat, preferred_element_type=jnp.float32)
        hidden = (jax.nn.silu(gate_val) * up_val).astype(jnp.bfloat16)
        return jnp.dot(hidden, down_mat, preferred_element_type=jnp.float32)
    expert_outputs = lax.map(one_expert, (w_gate, w_up, w_down, slot_table))
    picked = expert_outputs[route_flat, slot_index].reshape(TOKENS, 2, D)
    mixture = lax.optimization_barrier(jnp.sum(gate_weights.astype(jnp.float32)[:, :, None] * picked, axis=1))
    layer_out = (stream.astype(jnp.float32) + mixture).astype(jnp.bfloat16)
    return (attention_out, layer_out)
```

```python
import functools
import math

import jax
import jax.numpy as jnp
from jax import lax
from jax.experimental import pallas as pl
from jax.experimental.pallas import tpu as pltpu
from jax.sharding import PartitionSpec as P

Q_HEADS = 32
KV_HEADS = 8
HEAD_DIM = 128
EXPERTS = 8
CAP = 32
EPS = 1e-05
HIDE = -1e30
EMPTY = 63
META = 64
MESH = pl.DeviceIdType.MESH
VMEM = pltpu.VMEM


def whole(memory_space=VMEM):
    return pl.BlockSpec(memory_space=memory_space)


def greet(dp_peers, expert_peers):
    barrier = pltpu.get_barrier_semaphore()
    for peer in dp_peers:
        pl.semaphore_signal(barrier, inc=1, device_id={"dp": peer}, device_id_type=MESH)
    for peer in expert_peers:
        pl.semaphore_signal(barrier, inc=1, device_id={"expert": peer}, device_id_type=MESH)
    pl.semaphore_wait(barrier, len(dp_peers) + len(expert_peers))


def remote(src, dst, send, recv, axis, peer):
    return pltpu.make_async_remote_copy(
        src_ref=src, dst_ref=dst, send_sem=send, recv_sem=recv, device_id={axis: peer}, device_id_type=MESH
    )


def attention_kernel(
    n, n_e, kv_local, group,
    qx, keys, values, hot, residual,
    attention_out, gathered, meta,
    qall, so, sl, ro, rl,
    q_send, q_recv, o_send, o_recv, l_send, l_recv, z_send, z_recv, c_send, c_recv, s_send, s_recv,
):
    me, my_e = lax.axis_index("dp"), lax.axis_index("expert")
    rows, features = residual.shape
    half = n // 2
    chip, core = me // 2, me % 2
    sibling = chip * 2 + (1 - core)
    coeff = math.log2(math.e) / math.sqrt(HEAD_DIM)
    greet([(me + j) % n for j in range(1, n)], [(my_e + k) % n_e for k in range(1, n_e)])

    def q_copy(j, slot):
        return remote(qx, qall.at[slot], q_send.at[j], q_recv.at[j], "dp", (me + j) % n)

    for j in range(1, n):
        q_copy(j, me).start()
    qall[me] = qx[...]

    def o_copy(j):
        return remote(so.at[j], ro.at[j], o_send.at[j], o_recv.at[j], "dp", (me + n - j) % n)

    def l_copy(j):
        return remote(sl.at[j], rl.at[j], l_send.at[j], l_recv.at[j], "dp", (me + n - j) % n)

    lane = lax.broadcasted_iota(jnp.int32, (rows, 128), 1)

    def attend(j, carry):
        source = (me + n - j) % n

        @pl.when(j > 0)
        def _():
            q_copy(j, source).wait_recv()

        block = qall[source]
        side = block[:, features:]
        side = jnp.concatenate([side] * group, axis=0)
        logs = jnp.zeros((rows, 128), jnp.float32)
        for kv in range(kv_local):
            first = kv * group
            q = jnp.concatenate(
                [block[:, (first + g) * HEAD_DIM : (first + g + 1) * HEAD_DIM] for g in range(group)], axis=0
            )
            q = jnp.concatenate([q, side], axis=1)
            cut = slice(kv * HEAD_DIM, (kv + 1) * HEAD_DIM)
            k = jnp.concatenate([keys[:, cut], hot[...]], axis=1)
            scores = lax.dot_general(q, k, (((1,), (1,)), ((), ())), preferred_element_type=jnp.float32)
            top = jnp.max(scores, axis=1, keepdims=True)
            probs = jnp.exp2((scores - top) * coeff).astype(jnp.bfloat16)
            v = values[:, cut]
            v = jnp.concatenate([v, jnp.ones_like(v)], axis=1)
            out = jnp.dot(probs, v, preferred_element_type=jnp.float32)
            total = out[:, HEAD_DIM : HEAD_DIM + 1]
            out = (out[:, :HEAD_DIM] / total).astype(jnp.bfloat16)
            log = top * coeff + jnp.log(total) * math.log2(math.e)
            for g in range(group):
                part = slice(g * rows, (g + 1) * rows)
                so[j, :, (first + g) * HEAD_DIM : (first + g + 1) * HEAD_DIM] = out[part]
                logs = jnp.where(lane == first + g, log[part], logs)
        sl[j] = logs

        @pl.when(j > 0)
        def _():
            o_copy(j).start()
            l_copy(j).start()

        return carry

    lax.fori_loop(0, n, attend, 0)
    meta[...] = qall[:, :, features:]

    for j in range(1, n):
        l_copy(j).wait_recv()
        o_copy(j).wait_recv()
    logs = [sl[0]] + [rl[j] for j in range(1, n)]
    top = functools.reduce(jnp.maximum, logs)
    weights = [jnp.exp2(log - top) for log in logs]
    total = functools.reduce(jnp.add, weights)
    weights = [w / total for w in weights]
    for h in range(kv_local * group):
        cut = slice(h * HEAD_DIM, (h + 1) * HEAD_DIM)
        acc = weights[0][:, h : h + 1] * so[0, :, cut].astype(jnp.float32)
        for j in range(1, n):
            acc = acc + weights[j][:, h : h + 1] * ro[j, :, cut].astype(jnp.float32)
        attention_out[:, cut] = acc.astype(jnp.bfloat16)
        stream = (residual[:, cut].astype(jnp.float32) + acc).astype(jnp.bfloat16)
        column = pl.multiple_of(my_e * features + h * HEAD_DIM, HEAD_DIM)
        gathered[pl.ds(pl.multiple_of(me * rows, rows), rows), pl.ds(column, HEAD_DIM)] = stream

    def place(owner, k):
        column = (my_e + n_e - k) % n_e
        return gathered.at[
            pl.ds(pl.multiple_of(owner * rows, rows), rows),
            pl.ds(pl.multiple_of(column * features, features), features),
        ]

    def z_copy(k, slot):
        return remote(place(me, 0), slot, z_send.at[k], z_recv.at[k], "expert", (my_e + k) % n_e)

    def c_copy(j, k, slot):
        peer = ((chip + j) % half) * 2 + core
        return remote(place(me, k), slot, c_send.at[j, k], c_recv.at[j, k], "dp", peer)

    def s_copy(j, k, slot):
        owner = ((chip + half - j) % half) * 2 + core
        return remote(place(owner, k), slot, s_send.at[j, k], s_recv.at[j, k], "dp", sibling)

    for k in range(1, n_e):
        z_copy(k, place(me, 0)).start()
    for k in range(n_e):
        if k > 0:
            z_copy(k, place(me, k)).wait_recv()
        for j in range(1, half):
            c_copy(j, k, place(me, k)).start()
        s_copy(0, k, place(me, k)).start()
    for k in range(n_e):
        for j in range(1, half):
            owner = ((chip + half - j) % half) * 2 + core
            c_copy(j, k, place(owner, k)).wait_recv()
            s_copy(j, k, place(owner, k)).start()
    for k in range(n_e):
        for j in range(half):
            owner = ((chip + half - j) % half) * 2 + (1 - core)
            s_copy(j, k, place(owner, k)).wait_recv()
    for j in range(1, n):
        q_copy(j, me).wait_send()
        o_copy(j).wait_send()
        l_copy(j).wait_send()
    for k in range(n_e):
        if k > 0:
            z_copy(k, place(me, 0)).wait_send()
        for j in range(half):
            if j > 0:
                c_copy(j, k, place(me, k)).wait_send()
            s_copy(j, k, place(me, k)).wait_send()


def attend_and_gather(qx, keys, values, hot, residual, n, n_e):
    rows, features = residual.shape
    kv_local = keys.shape[1] // HEAD_DIM
    group = Q_HEADS // KV_HEADS
    half = n // 2
    bf16, f32 = jnp.bfloat16, jnp.float32
    dma = pltpu.SemaphoreType.DMA
    return pl.pallas_call(
        functools.partial(attention_kernel, n, n_e, kv_local, group),
        out_shape=(
            jax.ShapeDtypeStruct((rows, features), bf16),
            jax.ShapeDtypeStruct((n * rows, n_e * features), bf16),
            jax.ShapeDtypeStruct((n, rows, 128), bf16),
        ),
        in_specs=[whole()] * 5,
        out_specs=(whole(), whole(), whole()),
        scratch_shapes=[
            VMEM((n, rows, features + 128), bf16),
            VMEM((n, rows, features), bf16),
            VMEM((n, rows, 128), f32),
            VMEM((n, rows, features), bf16),
            VMEM((n, rows, 128), f32),
        ]
        + [dma((n,))] * 6
        + [dma((n_e,))] * 2
        + [dma((half, n_e))] * 4,
        compiler_params=pltpu.CompilerParams(
            collective_id=0, has_side_effects=True, vmem_limit_bytes=56 * 2**20
        ),
        name="attention_gather",
    )(qx, keys, values, hot, residual)


def expert_kernel(steps, chunk, stream, gain, target, weight, w_gate, w_up, w_down, out, rows_in, acc):
    x, f = pl.program_id(0), pl.program_id(1)
    tokens, width = stream.shape
    slots = acc.shape[0]
    per = slots // pl.num_programs(0)

    @pl.when((x == 0) & (f == 0))
    def _():
        spot = lax.broadcasted_iota(jnp.int32, (tokens, slots), 1)
        pick = (spot == target[:, 0:1]) | (spot == target[:, 1:2])
        pick = pick.astype(jnp.float32).astype(jnp.bfloat16)

        def norm(i, carry):
            cut = pl.ds(pl.multiple_of(i * 64, 64), 64)
            wide = stream[cut, :].astype(jnp.float32)
            inverse = lax.rsqrt(jnp.mean(wide * wide, axis=1, keepdims=True) + EPS)
            out[cut, :] = (wide * inverse * gain[...].astype(jnp.float32)).astype(jnp.bfloat16)
            return carry

        lax.fori_loop(0, tokens // 64, norm, 0)

        def choose(i, carry):
            cut = pl.ds(pl.multiple_of(i * chunk, chunk), chunk)
            rows_in[:, cut] = lax.dot_general(
                pick, out[:, cut], (((0,), (0,)), ((), ())), preferred_element_type=jnp.float32
            ).astype(jnp.bfloat16)
            return carry

        lax.fori_loop(0, width // chunk, choose, 0)

    mine = pl.ds(pl.multiple_of(x * per, per), per)
    data = rows_in[mine, :]
    gate = jnp.dot(data, w_gate[0], preferred_element_type=jnp.float32)
    up = jnp.dot(data, w_up[0], preferred_element_type=jnp.float32)
    hidden = (gate / (1.0 + jnp.exp(-gate)) * up).astype(jnp.bfloat16)

    def down(i, carry):
        cut = pl.ds(pl.multiple_of(i * chunk, chunk), chunk)
        term = jnp.dot(hidden, w_down[0, :, cut], preferred_element_type=jnp.float32)

        @pl.when(f == 0)
        def _():
            acc[mine, cut] = term

        @pl.when(f > 0)
        def _():
            acc[mine, cut] += term

        return carry

    lax.fori_loop(0, width // chunk, down, 0)

    @pl.when((x == pl.num_programs(0) - 1) & (f == steps - 1))
    def _():
        spot = lax.broadcasted_iota(jnp.int32, (tokens, slots), 1)
        mix = jnp.where(spot == target[:, 0:1], weight[:, 0:1], 0.0)
        mix = mix + jnp.where(spot == target[:, 1:2], weight[:, 1:2], 0.0)
        mix = mix.astype(jnp.bfloat16)

        def combine(i, carry):
            cut = pl.ds(pl.multiple_of(i * chunk, chunk), chunk)
            out[:, cut] = jnp.dot(
                mix, acc[:, cut].astype(jnp.bfloat16), preferred_element_type=jnp.float32
            ).astype(jnp.bfloat16)
            return carry

        lax.fori_loop(0, width // chunk, combine, 0)


def run_experts(stream, gain, target, weight, w_gate, w_up, w_down, slots):
    tokens, width = stream.shape
    local, _, hidden = w_gate.shape
    tile = 256 if hidden % 256 == 0 else 128
    steps = hidden // tile
    fixed = lambda x, f: (0, 0)
    once = pl.Buffered(1)
    return pl.pallas_call(
        functools.partial(expert_kernel, steps, 512),
        grid=(local, steps),
        out_shape=jax.ShapeDtypeStruct((tokens, width), jnp.bfloat16),
        in_specs=[
            pl.BlockSpec((tokens, width), fixed, pipeline_mode=once),
            pl.BlockSpec((1, width), fixed),
            pl.BlockSpec((tokens, 2), fixed),
            pl.BlockSpec((tokens, 2), fixed),
            pl.BlockSpec((1, width, tile), lambda x, f: (x, 0, f)),
            pl.BlockSpec((1, width, tile), lambda x, f: (x, 0, f)),
            pl.BlockSpec((1, tile, width), lambda x, f: (x, f, 0)),
        ],
        out_specs=pl.BlockSpec((tokens, width), fixed, pipeline_mode=once),
        scratch_shapes=[VMEM((slots, width), jnp.bfloat16), VMEM((slots, width), jnp.float32)],
        compiler_params=pltpu.CompilerParams(
            dimension_semantics=("arbitrary", "arbitrary"), vmem_limit_bytes=58 * 2**20
        ),
        name="experts",
    )(stream, gain, target, weight, w_gate, w_up, w_down)


def scatter_kernel(
    n, n_e, part, stream, out, buf_s, acc, buf_c, zsend, buf_z,
    s_send, s_recv, c_send, c_recv, z_send, z_recv,
):
    me, my_e = lax.axis_index("dp"), lax.axis_index("expert")
    rows, features = out.shape
    half = n // 2
    chip, core = me // 2, me % 2
    sibling = chip * 2 + (1 - core)
    greet(
        [((chip + j) % half) * 2 + core for j in range(1, half)] + [sibling],
        [(my_e + k) % n_e for k in range(1, n_e)],
    )

    def spot(j, k, side):
        owner = ((chip + j) % half) * 2 + side
        column = (my_e + k) % n_e
        return (
            pl.ds(pl.multiple_of(owner * rows, rows), rows),
            pl.ds(pl.multiple_of(column * features, features), features),
        )

    def s_copy(j, k):
        return remote(
            part.at[spot(j, k, 1 - core)], buf_s.at[j, k], s_send.at[j, k], s_recv.at[j, k], "dp", sibling
        )

    def c_copy(j, k):
        peer = ((chip + j) % half) * 2 + core
        return remote(acc.at[j, k], buf_c.at[j, k], c_send.at[j, k], c_recv.at[j, k], "dp", peer)

    def z_copy(k):
        return remote(zsend.at[k], buf_z.at[k], z_send.at[k], z_recv.at[k], "expert", (my_e + k) % n_e)

    far = [j for j in range(1, half)] + [0]
    columns = [k for k in range(1, n_e)] + [0]
    for k in columns:
        for j in far:
            s_copy(j, k).start()
    for k in columns:
        for j in far:
            s_copy(j, k).wait_recv()
            total = part[spot(j, k, core)].astype(jnp.float32) + buf_s[j, k].astype(jnp.float32)
            acc[j, k] = total.astype(jnp.bfloat16)
            if j > 0:
                c_copy(j, k).start()
    for k in columns:
        total = acc[0, k].astype(jnp.float32)
        for j in range(1, half):
            c_copy(j, k).wait_recv()
            total = total + buf_c[j, k].astype(jnp.float32)
        zsend[k] = total.astype(jnp.bfloat16)
        if k > 0:
            z_copy(k).start()
    total = zsend[0].astype(jnp.float32)
    for k in range(1, n_e):
        z_copy(k).wait_recv()
        total = total + buf_z[k].astype(jnp.float32)
    own = stream[spot(0, 0, core)].astype(jnp.float32)
    out[...] = (own + total).astype(jnp.bfloat16)
    for k in range(n_e):
        for j in range(half):
            s_copy(j, k).wait_send()
            if j > 0:
                c_copy(j, k).wait_send()
        if k > 0:
            z_copy(k).wait_send()


def sum_and_scatter(part, stream, n, n_e):
    rows, features = part.shape[0] // n, part.shape[1] // n_e
    half = n // 2
    bf16 = jnp.bfloat16
    dma = pltpu.SemaphoreType.DMA
    return pl.pallas_call(
        functools.partial(scatter_kernel, n, n_e),
        out_shape=jax.ShapeDtypeStruct((rows, features), bf16),
        in_specs=[whole()] * 2,
        out_specs=whole(),
        scratch_shapes=[
            VMEM((half, n_e, rows, features), bf16),
            VMEM((half, n_e, rows, features), bf16),
            VMEM((half, n_e, rows, features), bf16),
            VMEM((n_e, rows, features), bf16),
            VMEM((n_e, rows, features), bf16),
        ]
        + [dma((half, n_e))] * 4
        + [dma((n_e,))] * 2,
        compiler_params=pltpu.CompilerParams(
            collective_id=1, has_side_effects=True, vmem_limit_bytes=48 * 2**20
        ),
        name="sum_scatter",
    )(part, stream)


def body(
    residual, queries, cache_keys, cache_values, node_of_position, parent, leaf_ids, routes,
    gate_weights, norm_gain, w_gate, w_up, w_down,
):
    n, n_e = lax.axis_size("dp"), lax.axis_size("expert")
    rows = queries.shape[0]
    nodes = parent.shape[0]
    local = w_gate.shape[0]
    bf16 = jnp.bfloat16
    side = jnp.arange(128, dtype=jnp.int32)[None, :]
    node_range = jnp.arange(nodes, dtype=jnp.int32)[None, :]

    def parent_of(ids):
        return jnp.sum(jnp.where(ids[:, None] == node_range, parent[None, :], 0), axis=1)

    middle = parent_of(leaf_ids)
    upper = parent_of(middle)
    seen = (side == leaf_ids[:, None]) | (side == middle[:, None]) | (side == upper[:, None])

    flat = routes.reshape(-1)
    same = flat[:, None] == flat[None, :]
    order = jnp.arange(flat.shape[0], dtype=jnp.int32)
    ranks = jnp.sum((same & (order[None, :] < order[:, None])).astype(jnp.int32), axis=1).reshape(rows, 2)
    values = jnp.where(seen, 0.0, HIDE)
    info = jnp.concatenate(
        [routes.astype(jnp.float32), ranks.astype(jnp.float32), gate_weights.astype(jnp.float32)], axis=1
    )
    info = jnp.pad(info, ((0, 0), (META, 128 - META - 6)))
    values = jnp.where(side >= META, info, values).astype(bf16)
    qx = jnp.concatenate([queries, values], axis=1)
    column = jnp.where(node_of_position < 0, EMPTY, node_of_position)
    hot = (column[:, None] == side).astype(bf16)

    attention_out, stream, meta = attend_and_gather(qx, cache_keys, cache_values, hot, residual, n, n_e)

    info = meta[:, :, META : META + 6].astype(jnp.float32).reshape(n * rows, 6)
    expert = info[:, 0:2].astype(jnp.int32) - lax.axis_index("expert") * local
    owner = jnp.arange(n * rows, dtype=jnp.int32)[:, None] // rows
    target = expert * (n * CAP) + owner * CAP + info[:, 2:4].astype(jnp.int32)
    target = jnp.where((expert >= 0) & (expert < local), target, -1)
    part = run_experts(
        stream, norm_gain.reshape(1, -1), target, info[:, 4:6], w_gate, w_up, w_down, local * n * CAP
    )
    layer_out = sum_and_scatter(part, stream, n, n_e)
    return attention_out, layer_out


def solution(mesh):
    in_specs = (
        P("dp", "expert"),
        P("dp", "expert"),
        P("dp", "expert"),
        P("dp", "expert"),
        P("dp"),
        P(),
        P("dp"),
        P("dp", None),
        P("dp", None),
        P(),
        P("expert", None, "dp"),
        P("expert", None, "dp"),
        P("expert", "dp", None),
    )
    out_specs = (P("dp", "expert"), P("dp", "expert"))
    return jax.shard_map(body, mesh=mesh, in_specs=in_specs, out_specs=out_specs, check_vma=False)
```

```python
import functools
import math

import jax
import jax.numpy as jnp
from jax import lax
from jax.experimental import pallas as pl
from jax.experimental.pallas import tpu as pltpu
from jax.sharding import PartitionSpec as P

Q_HEADS = 32
KV_HEADS = 8
HEAD_DIM = 128
EXPERTS = 8
CAP = 32
EPS = 1e-05
HIDE = -1e30
EMPTY = 63
META = 64
MESH = pl.DeviceIdType.MESH
VMEM = pltpu.VMEM


def whole(memory_space=VMEM):
    return pl.BlockSpec(memory_space=memory_space)


def greet(dp_peers, expert_peers):
    barrier = pltpu.get_barrier_semaphore()
    for peer in dp_peers:
        pl.semaphore_signal(barrier, inc=1, device_id={"dp": peer}, device_id_type=MESH)
    for peer in expert_peers:
        pl.semaphore_signal(barrier, inc=1, device_id={"expert": peer}, device_id_type=MESH)
    return lambda: pl.semaphore_wait(barrier, len(dp_peers) + len(expert_peers))


def side_values(parent, leaf, routes, gate_weights):
    rows = leaf.shape[1]

    def parent_of(ids):
        found = jnp.zeros_like(ids)
        for node in range(parent.shape[0]):
            found = jnp.where(ids == node, parent[node], found)
        return found

    own = leaf[...]
    middle = parent_of(own)
    upper = parent_of(middle)
    place = lax.broadcasted_iota(jnp.int32, (128, rows), 0)
    seen = (place == own) | (place == middle) | (place == upper)
    named = [routes[0:1, :], routes[1:2, :]]
    expert = lax.broadcasted_iota(jnp.int32, (EXPERTS, rows), 0)
    hot = ((expert == named[0]) | (expert == named[1])).astype(jnp.float32)
    before = lax.broadcasted_iota(jnp.int32, (rows, rows), 0) < lax.broadcasted_iota(jnp.int32, (rows, rows), 1)
    count = jnp.dot(hot, before.astype(jnp.float32), preferred_element_type=jnp.float32)
    ranks = [jnp.sum(jnp.where(expert == e, count, 0.0), axis=0, keepdims=True) for e in named]
    weights = gate_weights[...].astype(jnp.float32)
    info = [e.astype(jnp.float32) for e in named] + ranks + [weights[0:1, :], weights[1:2, :]]
    values = jnp.where(place >= META, 0.0, jnp.where(seen, 0.0, HIDE))
    for i, row in enumerate(info):
        values = jnp.where(place == META + i, row, values)
    return values.T.astype(jnp.bfloat16)


def remote(src, dst, send, recv, axis, peer):
    return pltpu.make_async_remote_copy(
        src_ref=src, dst_ref=dst, send_sem=send, recv_sem=recv, device_id={axis: peer}, device_id_type=MESH
    )


def attention_kernel(
    n, n_e, kv_local, group,
    queries, parent, leaf, routes, gate_weights, node, keys, values, residual,
    attention_out, gathered, meta,
    hot, qall, so, sl, ro, rl,
    q_send, q_recv, o_send, o_recv, l_send, l_recv, z_send, z_recv, c_send, c_recv, s_send, s_recv,
):
    me, my_e = lax.axis_index("dp"), lax.axis_index("expert")
    rows, features = residual.shape
    half = n // 2
    chip, core = me // 2, me % 2
    sibling = chip * 2 + (1 - core)
    coeff = math.log2(math.e) / math.sqrt(HEAD_DIM)
    wait_all = greet([(me + j) % n for j in range(1, n)], [(my_e + k) % n_e for k in range(1, n_e)])
    qall[me] = jnp.concatenate([queries[...], side_values(parent, leaf, routes, gate_weights)], axis=1)
    wait_all()

    def q_copy(j, slot):
        return remote(qall.at[me], qall.at[slot], q_send.at[j], q_recv.at[j], "dp", (me + j) % n)

    for j in range(1, n):
        q_copy(j, me).start()
    node_row = jnp.where(node[...] < 0, EMPTY, node[...])
    spread = lax.broadcasted_iota(jnp.int32, (128, node.shape[1]), 0) == node_row
    hot[...] = spread.astype(jnp.float32).T.astype(jnp.bfloat16)

    def o_copy(j):
        return remote(so.at[j], ro.at[j], o_send.at[j], o_recv.at[j], "dp", (me + n - j) % n)

    def l_copy(j):
        return remote(sl.at[j], rl.at[j], l_send.at[j], l_recv.at[j], "dp", (me + n - j) % n)

    lane = lax.broadcasted_iota(jnp.int32, (rows, 128), 1)

    def attend(j, carry):
        source = (me + n - j) % n

        @pl.when(j > 0)
        def _():
            q_copy(j, source).wait_recv()

        block = qall[source]
        side = block[:, features:]
        side = jnp.concatenate([side] * group, axis=0)
        logs = jnp.zeros((rows, 128), jnp.float32)
        for kv in range(kv_local):
            first = kv * group
            q = jnp.concatenate(
                [block[:, (first + g) * HEAD_DIM : (first + g + 1) * HEAD_DIM] for g in range(group)], axis=0
            )
            q = jnp.concatenate([q, side], axis=1)
            cut = slice(kv * HEAD_DIM, (kv + 1) * HEAD_DIM)
            k = jnp.concatenate([keys[:, cut], hot[...]], axis=1)
            scores = lax.dot_general(q, k, (((1,), (1,)), ((), ())), preferred_element_type=jnp.float32)
            top = jnp.max(scores, axis=1, keepdims=True)
            probs = jnp.exp2((scores - top) * coeff).astype(jnp.bfloat16)
            v = values[:, cut]
            v = jnp.concatenate([v, jnp.ones_like(v)], axis=1)
            out = jnp.dot(probs, v, preferred_element_type=jnp.float32)
            total = out[:, HEAD_DIM : HEAD_DIM + 1]
            out = (out[:, :HEAD_DIM] / total).astype(jnp.bfloat16)
            log = top * coeff + jnp.log(total) * math.log2(math.e)
            for g in range(group):
                part = slice(g * rows, (g + 1) * rows)
                so[j, :, (first + g) * HEAD_DIM : (first + g + 1) * HEAD_DIM] = out[part]
                logs = jnp.where(lane == first + g, log[part], logs)
        sl[j] = logs

        @pl.when(j > 0)
        def _():
            o_copy(j).start()
            l_copy(j).start()

        return carry

    lax.fori_loop(0, n, attend, 0)
    meta[...] = qall[:, :, features:]

    for j in range(1, n):
        l_copy(j).wait_recv()
        o_copy(j).wait_recv()
    logs = [sl[0]] + [rl[j] for j in range(1, n)]
    top = functools.reduce(jnp.maximum, logs)
    weights = [jnp.exp2(log - top) for log in logs]
    total = functools.reduce(jnp.add, weights)
    weights = [w / total for w in weights]
    for h in range(kv_local * group):
        cut = slice(h * HEAD_DIM, (h + 1) * HEAD_DIM)
        acc = weights[0][:, h : h + 1] * so[0, :, cut].astype(jnp.float32)
        for j in range(1, n):
            acc = acc + weights[j][:, h : h + 1] * ro[j, :, cut].astype(jnp.float32)
        attention_out[:, cut] = acc.astype(jnp.bfloat16)
        stream = (residual[:, cut].astype(jnp.float32) + acc).astype(jnp.bfloat16)
        column = pl.multiple_of(my_e * features + h * HEAD_DIM, HEAD_DIM)
        gathered[pl.ds(pl.multiple_of(me * rows, rows), rows), pl.ds(column, HEAD_DIM)] = stream

    def place(owner, k):
        column = (my_e + n_e - k) % n_e
        return gathered.at[
            pl.ds(pl.multiple_of(owner * rows, rows), rows),
            pl.ds(pl.multiple_of(column * features, features), features),
        ]

    def z_copy(k, slot):
        return remote(place(me, 0), slot, z_send.at[k], z_recv.at[k], "expert", (my_e + k) % n_e)

    def c_copy(j, k, slot):
        peer = ((chip + j) % half) * 2 + core
        return remote(place(me, k), slot, c_send.at[j, k], c_recv.at[j, k], "dp", peer)

    def s_copy(j, k, slot):
        owner = ((chip + half - j) % half) * 2 + core
        return remote(place(owner, k), slot, s_send.at[j, k], s_recv.at[j, k], "dp", sibling)

    for k in range(1, n_e):
        z_copy(k, place(me, 0)).start()
    for k in range(n_e):
        if k > 0:
            z_copy(k, place(me, k)).wait_recv()
        for j in range(1, half):
            c_copy(j, k, place(me, k)).start()
        s_copy(0, k, place(me, k)).start()
    for k in range(n_e):
        for j in range(1, half):
            owner = ((chip + half - j) % half) * 2 + core
            c_copy(j, k, place(owner, k)).wait_recv()
            s_copy(j, k, place(owner, k)).start()
    for k in range(n_e):
        for j in range(half):
            owner = ((chip + half - j) % half) * 2 + (1 - core)
            s_copy(j, k, place(owner, k)).wait_recv()
    for j in range(1, n):
        q_copy(j, me).wait_send()
        o_copy(j).wait_send()
        l_copy(j).wait_send()
    for k in range(n_e):
        if k > 0:
            z_copy(k, place(me, 0)).wait_send()
        for j in range(half):
            if j > 0:
                c_copy(j, k, place(me, k)).wait_send()
            s_copy(j, k, place(me, k)).wait_send()


def attend_and_gather(queries, parent, leaf, routes, gate_weights, node, keys, values, residual, n, n_e):
    rows, features = residual.shape
    kv_local = keys.shape[1] // HEAD_DIM
    group = Q_HEADS // KV_HEADS
    half = n // 2
    bf16, f32 = jnp.bfloat16, jnp.float32
    dma = pltpu.SemaphoreType.DMA
    return pl.pallas_call(
        functools.partial(attention_kernel, n, n_e, kv_local, group),
        out_shape=(
            jax.ShapeDtypeStruct((rows, features), bf16),
            jax.ShapeDtypeStruct((n * rows, n_e * features), bf16),
            jax.ShapeDtypeStruct((n, rows, 128), bf16),
        ),
        in_specs=[whole(), whole(pltpu.SMEM)] + [whole()] * 7,
        out_specs=(whole(), whole(), whole()),
        scratch_shapes=[
            VMEM((keys.shape[0], 128), bf16),
            VMEM((n, rows, features + 128), bf16),
            VMEM((n, rows, features), bf16),
            VMEM((n, rows, 128), f32),
            VMEM((n, rows, features), bf16),
            VMEM((n, rows, 128), f32),
        ]
        + [dma((n,))] * 6
        + [dma((n_e,))] * 2
        + [dma((half, n_e))] * 4,
        compiler_params=pltpu.CompilerParams(
            collective_id=0, has_side_effects=True, vmem_limit_bytes=56 * 2**20
        ),
        name="attention_gather",
    )(queries, parent, leaf, routes, gate_weights, node, keys, values, residual)


def expert_kernel(
    k_steps, rows, stream, gain, meta, w_gate, w_up, w_down, out,
    inverse, pick, mix, gate, up, hidden, outs,
):
    x, f = pl.program_id(0), pl.program_id(1)
    tokens, width = stream.shape
    local, per, _ = outs.shape
    tile = w_gate.shape[1]
    columns = w_down.shape[2]
    base = lax.axis_index("expert") * local

    def slot_keys(values, owner):
        return [
            (values[i].astype(jnp.int32) - base, owner * CAP + values[2 + i].astype(jnp.int32)) for i in range(2)
        ]

    @pl.when((x == 0) & (f == 0))
    def _():
        def square(i, carry):
            cut = pl.ds(pl.multiple_of(i * 64, 64), 64)
            wide = stream[cut, :].astype(jnp.float32)
            mean = jnp.mean(wide * wide, axis=1, keepdims=True)
            inverse[cut, :] = jnp.broadcast_to(lax.rsqrt(mean + EPS), (64, 128))
            return carry

        lax.fori_loop(0, tokens // 64, square, 0)
        info = meta[...].astype(jnp.float32)
        values = [info[:, META + i : META + i + 1] for i in range(6)]
        owner = lax.broadcasted_iota(jnp.int32, (tokens, 1), 0) // rows
        spot = lax.broadcasted_iota(jnp.int32, (tokens, local * per), 1)
        total = jnp.zeros((tokens, local * per), jnp.float32)
        for i, (expert, slot) in enumerate(slot_keys(values, owner)):
            target = jnp.where((expert >= 0) & (expert < local), expert * per + slot, -1)
            total = total + jnp.where(spot == target, values[4 + i], 0.0)
        mix[...] = total.astype(jnp.bfloat16)

    @pl.when(f == 0)
    def _():
        info = meta[...].astype(jnp.float32).T
        values = [info[META + i : META + i + 1, :] for i in range(4)]
        owner = lax.broadcasted_iota(jnp.int32, (1, tokens), 1) // rows
        spot = lax.broadcasted_iota(jnp.int32, (per, tokens), 0)
        hits = [spot == jnp.where(expert == x, slot, -1) for expert, slot in slot_keys(values, owner)]
        pick[...] = (hits[0] | hits[1]).astype(jnp.float32).astype(jnp.bfloat16)

    @pl.when(f < k_steps)
    def _():
        cut = pl.ds(pl.multiple_of(f * tile, tile), tile)
        wide = stream[:, cut].astype(jnp.float32)
        normed = (wide * inverse[:, 0:1] * gain[:, cut].astype(jnp.float32)).astype(jnp.bfloat16)
        data = jnp.dot(pick[...], normed, preferred_element_type=jnp.float32).astype(jnp.bfloat16)
        gate_term = jnp.dot(data, w_gate[0], preferred_element_type=jnp.float32)
        up_term = jnp.dot(data, w_up[0], preferred_element_type=jnp.float32)

        @pl.when(f == 0)
        def _():
            gate[...] = gate_term
            up[...] = up_term

        @pl.when(f > 0)
        def _():
            gate[...] += gate_term
            up[...] += up_term

    @pl.when(f == k_steps - 1)
    def _():
        value = gate[...]
        hidden[...] = (value / (1.0 + jnp.exp(-value)) * up[...]).astype(jnp.bfloat16)

    @pl.when(f >= k_steps)
    def _():
        cut = pl.ds(pl.multiple_of((f - k_steps) * columns, columns), columns)
        term = jnp.dot(hidden[...], w_down[0], preferred_element_type=jnp.float32).astype(jnp.bfloat16)
        outs[x, :, cut] = term

        @pl.when(x == local - 1)
        def _():
            both = outs[:, :, cut].reshape(local * per, columns)
            out[:, cut] = jnp.dot(mix[...], both, preferred_element_type=jnp.float32).astype(jnp.bfloat16)


def run_experts(stream, gain, meta, w_gate, w_up, w_down, rows):
    tokens, width = stream.shape
    local, _, hidden = w_gate.shape
    per = tokens // rows * CAP
    tile = 512
    k_steps = d_steps = width // tile
    bf16, f32 = jnp.bfloat16, jnp.float32
    fixed = lambda x, f: (0, 0)
    wide = lambda x, f: (x, jnp.minimum(f, k_steps - 1), 0)
    once = pl.Buffered(1)
    return pl.pallas_call(
        functools.partial(expert_kernel, k_steps, rows),
        grid=(local, k_steps + d_steps),
        out_shape=jax.ShapeDtypeStruct((tokens, width), bf16),
        in_specs=[
            pl.BlockSpec((tokens, width), fixed, pipeline_mode=once),
            pl.BlockSpec((1, width), fixed),
            pl.BlockSpec((tokens, 128), fixed),
            pl.BlockSpec((1, tile, hidden), wide),
            pl.BlockSpec((1, tile, hidden), wide),
            pl.BlockSpec((1, hidden, tile), lambda x, f: (x, 0, jnp.maximum(f - k_steps, 0))),
        ],
        out_specs=pl.BlockSpec((tokens, width), fixed, pipeline_mode=once),
        scratch_shapes=[
            VMEM((tokens, 128), f32),
            VMEM((per, tokens), bf16),
            VMEM((tokens, local * per), bf16),
            VMEM((per, hidden), f32),
            VMEM((per, hidden), f32),
            VMEM((per, hidden), bf16),
            VMEM((local, per, width), bf16),
        ],
        compiler_params=pltpu.CompilerParams(
            dimension_semantics=("arbitrary", "arbitrary"), vmem_limit_bytes=58 * 2**20
        ),
        name="experts",
    )(stream, gain, meta, w_gate, w_up, w_down)


def scatter_kernel(
    n, n_e, part, stream, out, buf_s, acc, buf_c, zsend, buf_z,
    s_send, s_recv, c_send, c_recv, z_send, z_recv,
):
    me, my_e = lax.axis_index("dp"), lax.axis_index("expert")
    rows, features = out.shape
    half = n // 2
    chip, core = me // 2, me % 2
    sibling = chip * 2 + (1 - core)
    wait_all = greet(
        [((chip + j) % half) * 2 + core for j in range(1, half)] + [sibling],
        [(my_e + k) % n_e for k in range(1, n_e)],
    )
    wait_all()

    def spot(j, k, side):
        owner = ((chip + j) % half) * 2 + side
        column = (my_e + k) % n_e
        return (
            pl.ds(pl.multiple_of(owner * rows, rows), rows),
            pl.ds(pl.multiple_of(column * features, features), features),
        )

    def s_copy(j, k):
        return remote(
            part.at[spot(j, k, 1 - core)], buf_s.at[j, k], s_send.at[j, k], s_recv.at[j, k], "dp", sibling
        )

    def c_copy(j, k):
        peer = ((chip + j) % half) * 2 + core
        return remote(acc.at[j, k], buf_c.at[j, k], c_send.at[j, k], c_recv.at[j, k], "dp", peer)

    def z_copy(k):
        return remote(zsend.at[k], buf_z.at[k], z_send.at[k], z_recv.at[k], "expert", (my_e + k) % n_e)

    far = [j for j in range(1, half)] + [0]
    columns = [k for k in range(1, n_e)] + [0]
    for k in columns:
        for j in far:
            s_copy(j, k).start()
    for k in columns:
        for j in far:
            s_copy(j, k).wait_recv()
            total = part[spot(j, k, core)].astype(jnp.float32) + buf_s[j, k].astype(jnp.float32)
            acc[j, k] = total.astype(jnp.bfloat16)
            if j > 0:
                c_copy(j, k).start()
    for k in columns:
        total = acc[0, k].astype(jnp.float32)
        for j in range(1, half):
            c_copy(j, k).wait_recv()
            total = total + buf_c[j, k].astype(jnp.float32)
        zsend[k] = total.astype(jnp.bfloat16)
        if k > 0:
            z_copy(k).start()
    total = zsend[0].astype(jnp.float32)
    for k in range(1, n_e):
        z_copy(k).wait_recv()
        total = total + buf_z[k].astype(jnp.float32)
    own = stream[spot(0, 0, core)].astype(jnp.float32)
    out[...] = (own + total).astype(jnp.bfloat16)
    for k in range(n_e):
        for j in range(half):
            s_copy(j, k).wait_send()
            if j > 0:
                c_copy(j, k).wait_send()
        if k > 0:
            z_copy(k).wait_send()


def sum_and_scatter(part, stream, n, n_e):
    rows, features = part.shape[0] // n, part.shape[1] // n_e
    half = n // 2
    bf16 = jnp.bfloat16
    dma = pltpu.SemaphoreType.DMA
    return pl.pallas_call(
        functools.partial(scatter_kernel, n, n_e),
        out_shape=jax.ShapeDtypeStruct((rows, features), bf16),
        in_specs=[whole()] * 2,
        out_specs=whole(),
        scratch_shapes=[
            VMEM((half, n_e, rows, features), bf16),
            VMEM((half, n_e, rows, features), bf16),
            VMEM((half, n_e, rows, features), bf16),
            VMEM((n_e, rows, features), bf16),
            VMEM((n_e, rows, features), bf16),
        ]
        + [dma((half, n_e))] * 4
        + [dma((n_e,))] * 2,
        compiler_params=pltpu.CompilerParams(
            collective_id=1, has_side_effects=True, vmem_limit_bytes=48 * 2**20
        ),
        name="sum_scatter",
    )(part, stream)


def body(
    residual, queries, cache_keys, cache_values, node_of_position, parent, leaf_ids, routes,
    gate_weights, norm_gain, w_gate, w_up, w_down,
):
    n, n_e = lax.axis_size("dp"), lax.axis_size("expert")
    rows = queries.shape[0]
    attention_out, stream, meta = attend_and_gather(
        queries, parent, leaf_ids.reshape(1, -1), routes.T, gate_weights.T, node_of_position.reshape(1, -1),
        cache_keys, cache_values, residual, n, n_e,
    )
    part = run_experts(
        stream, norm_gain.reshape(1, -1), meta.reshape(n * rows, 128), w_gate, w_up, w_down, rows
    )
    layer_out = sum_and_scatter(part, stream, n, n_e)
    return attention_out, layer_out


def solution(mesh):
    in_specs = (
        P("dp", "expert"),
        P("dp", "expert"),
        P("dp", "expert"),
        P("dp", "expert"),
        P("dp"),
        P(),
        P("dp"),
        P("dp", None),
        P("dp", None),
        P(),
        P("expert", None, "dp"),
        P("expert", None, "dp"),
        P("expert", "dp", None),
    )
    out_specs = (P("dp", "expert"), P("dp", "expert"))
    return jax.shard_map(body, mesh=mesh, in_specs=in_specs, out_specs=out_specs, check_vma=False)
```

```python
import functools
import math

import jax
import jax.numpy as jnp
from jax import lax
from jax.experimental import pallas as pl
from jax.experimental.pallas import tpu as pltpu
from jax.sharding import PartitionSpec as P

Q_HEADS = 32
KV_HEADS = 8
HEAD_DIM = 128
EXPERTS = 8
CAP = 32
EPS = 1e-05
HIDE = -1e30
EMPTY = 63
META = 64
MESH = pl.DeviceIdType.MESH
VMEM = pltpu.VMEM


def whole(memory_space=VMEM):
    return pl.BlockSpec(memory_space=memory_space)


def greet(dp_peers, expert_peers):
    barrier = pltpu.get_barrier_semaphore()
    for peer in dp_peers:
        pl.semaphore_signal(barrier, inc=1, device_id={"dp": peer}, device_id_type=MESH)
    for peer in expert_peers:
        pl.semaphore_signal(barrier, inc=1, device_id={"expert": peer}, device_id_type=MESH)
    return lambda: pl.semaphore_wait(barrier, len(dp_peers) + len(expert_peers))


def side_values(parent, leaf, routes, gate_weights):
    rows = leaf.shape[1]

    def parent_of(ids):
        found = jnp.zeros_like(ids)
        for node in range(parent.shape[0]):
            found = jnp.where(ids == node, parent[node], found)
        return found

    own = leaf[...]
    middle = parent_of(own)
    upper = parent_of(middle)
    place = lax.broadcasted_iota(jnp.int32, (128, rows), 0)
    seen = (place == own) | (place == middle) | (place == upper)
    named = [routes[0:1, :], routes[1:2, :]]
    expert = lax.broadcasted_iota(jnp.int32, (EXPERTS, rows), 0)
    hot = ((expert == named[0]) | (expert == named[1])).astype(jnp.float32)
    before = lax.broadcasted_iota(jnp.int32, (rows, rows), 0) < lax.broadcasted_iota(jnp.int32, (rows, rows), 1)
    count = jnp.dot(hot, before.astype(jnp.float32), preferred_element_type=jnp.float32)
    ranks = [jnp.sum(jnp.where(expert == e, count, 0.0), axis=0, keepdims=True) for e in named]
    weights = gate_weights[...].astype(jnp.float32)
    info = [e.astype(jnp.float32) for e in named] + ranks + [weights[0:1, :], weights[1:2, :]]
    values = jnp.where(place >= META, 0.0, jnp.where(seen, 0.0, HIDE))
    for i, row in enumerate(info):
        values = jnp.where(place == META + i, row, values)
    return values.T.astype(jnp.bfloat16)


def remote(src, dst, send, recv, axis, peer):
    return pltpu.make_async_remote_copy(
        src_ref=src, dst_ref=dst, send_sem=send, recv_sem=recv, device_id={axis: peer}, device_id_type=MESH
    )


def attention_kernel(
    n, n_e, kv_local, group,
    queries, parent, leaf, routes, gate_weights, node, keys, values, residual,
    attention_out, gathered, meta,
    hot, qall, so, sl, ro, rl,
    q_send, q_recv, o_send, o_recv, l_send, l_recv, z_send, z_recv, c_send, c_recv, s_send, s_recv,
):
    me, my_e = lax.axis_index("dp"), lax.axis_index("expert")
    rows, features = residual.shape
    half = n // 2
    chip, core = me // 2, me % 2
    sibling = chip * 2 + (1 - core)
    coeff = math.log2(math.e) / math.sqrt(HEAD_DIM)
    wait_all = greet([(me + j) % n for j in range(1, n)], [(my_e + k) % n_e for k in range(1, n_e)])
    qall[me] = jnp.concatenate([queries[...], side_values(parent, leaf, routes, gate_weights)], axis=1)
    wait_all()

    def q_copy(j, slot):
        return remote(qall.at[me], qall.at[slot], q_send.at[j], q_recv.at[j], "dp", (me + j) % n)

    for j in range(1, n):
        q_copy(j, me).start()
    node_row = jnp.where(node[...] < 0, EMPTY, node[...])
    spread = lax.broadcasted_iota(jnp.int32, (128, node.shape[1]), 0) == node_row
    hot[...] = spread.astype(jnp.float32).T.astype(jnp.bfloat16)

    def o_copy(j):
        return remote(so.at[j], ro.at[j], o_send.at[j], o_recv.at[j], "dp", (me + n - j) % n)

    def l_copy(j):
        return remote(sl.at[j], rl.at[j], l_send.at[j], l_recv.at[j], "dp", (me + n - j) % n)

    lane = lax.broadcasted_iota(jnp.int32, (rows, 128), 1)

    def attend(j, carry):
        source = (me + n - j) % n

        @pl.when(j > 0)
        def _():
            q_copy(j, source).wait_recv()

        block = qall[source]
        side = block[:, features:]
        side = jnp.concatenate([side] * group, axis=0)
        logs = jnp.zeros((rows, 128), jnp.float32)
        for kv in range(kv_local):
            first = kv * group
            q = jnp.concatenate(
                [block[:, (first + g) * HEAD_DIM : (first + g + 1) * HEAD_DIM] for g in range(group)], axis=0
            )
            q = jnp.concatenate([q, side], axis=1)
            cut = slice(kv * HEAD_DIM, (kv + 1) * HEAD_DIM)
            k = jnp.concatenate([keys[:, cut], hot[...]], axis=1)
            scores = lax.dot_general(q, k, (((1,), (1,)), ((), ())), preferred_element_type=jnp.float32)
            top = jnp.max(scores, axis=1, keepdims=True)
            probs = jnp.exp2((scores - top) * coeff).astype(jnp.bfloat16)
            v = values[:, cut]
            v = jnp.concatenate([v, jnp.ones_like(v)], axis=1)
            out = jnp.dot(probs, v, preferred_element_type=jnp.float32)
            total = out[:, HEAD_DIM : HEAD_DIM + 1]
            out = (out[:, :HEAD_DIM] / total).astype(jnp.bfloat16)
            log = top * coeff + jnp.log(total) * math.log2(math.e)
            for g in range(group):
                part = slice(g * rows, (g + 1) * rows)
                so[j, :, (first + g) * HEAD_DIM : (first + g + 1) * HEAD_DIM] = out[part]
                logs = jnp.where(lane == first + g, log[part], logs)
        sl[j] = logs

        @pl.when(j > 0)
        def _():
            o_copy(j).start()
            l_copy(j).start()

        return carry

    lax.fori_loop(0, n, attend, 0)
    meta[...] = qall[:, :, features:]

    for j in range(1, n):
        l_copy(j).wait_recv()
        o_copy(j).wait_recv()
    logs = [sl[0]] + [rl[j] for j in range(1, n)]
    top = functools.reduce(jnp.maximum, logs)
    weights = [jnp.exp2(log - top) for log in logs]
    total = functools.reduce(jnp.add, weights)
    weights = [w / total for w in weights]
    for h in range(kv_local * group):
        cut = slice(h * HEAD_DIM, (h + 1) * HEAD_DIM)
        acc = weights[0][:, h : h + 1] * so[0, :, cut].astype(jnp.float32)
        for j in range(1, n):
            acc = acc + weights[j][:, h : h + 1] * ro[j, :, cut].astype(jnp.float32)
        attention_out[:, cut] = acc.astype(jnp.bfloat16)
        stream = (residual[:, cut].astype(jnp.float32) + acc).astype(jnp.bfloat16)
        column = pl.multiple_of(my_e * features + h * HEAD_DIM, HEAD_DIM)
        gathered[pl.ds(pl.multiple_of(me * rows, rows), rows), pl.ds(column, HEAD_DIM)] = stream

    def place(owner, k):
        column = (my_e + n_e - k) % n_e
        return gathered.at[
            pl.ds(pl.multiple_of(owner * rows, rows), rows),
            pl.ds(pl.multiple_of(column * features, features), features),
        ]

    def z_copy(k, slot):
        return remote(place(me, 0), slot, z_send.at[k], z_recv.at[k], "expert", (my_e + k) % n_e)

    def c_copy(j, k, slot):
        peer = ((chip + j) % half) * 2 + core
        return remote(place(me, k), slot, c_send.at[j, k], c_recv.at[j, k], "dp", peer)

    def s_copy(j, k, slot):
        owner = ((chip + half - j) % half) * 2 + core
        return remote(place(owner, k), slot, s_send.at[j, k], s_recv.at[j, k], "dp", sibling)

    for k in range(1, n_e):
        z_copy(k, place(me, 0)).start()
    for k in range(n_e):
        if k > 0:
            z_copy(k, place(me, k)).wait_recv()
        for j in range(1, half):
            c_copy(j, k, place(me, k)).start()
        s_copy(0, k, place(me, k)).start()
    for k in range(n_e):
        for j in range(1, half):
            owner = ((chip + half - j) % half) * 2 + core
            c_copy(j, k, place(owner, k)).wait_recv()
            s_copy(j, k, place(owner, k)).start()
    for k in range(n_e):
        for j in range(half):
            owner = ((chip + half - j) % half) * 2 + (1 - core)
            s_copy(j, k, place(owner, k)).wait_recv()
    for j in range(1, n):
        q_copy(j, me).wait_send()
        o_copy(j).wait_send()
        l_copy(j).wait_send()
    for k in range(n_e):
        if k > 0:
            z_copy(k, place(me, 0)).wait_send()
        for j in range(half):
            if j > 0:
                c_copy(j, k, place(me, k)).wait_send()
            s_copy(j, k, place(me, k)).wait_send()


def attend_and_gather(queries, parent, leaf, routes, gate_weights, node, keys, values, residual, n, n_e):
    rows, features = residual.shape
    kv_local = keys.shape[1] // HEAD_DIM
    group = Q_HEADS // KV_HEADS
    half = n // 2
    bf16, f32 = jnp.bfloat16, jnp.float32
    dma = pltpu.SemaphoreType.DMA
    return pl.pallas_call(
        functools.partial(attention_kernel, n, n_e, kv_local, group),
        out_shape=(
            jax.ShapeDtypeStruct((rows, features), bf16),
            jax.ShapeDtypeStruct((n * rows, n_e * features), bf16),
            jax.ShapeDtypeStruct((n, rows, 128), bf16),
        ),
        in_specs=[whole(), whole(pltpu.SMEM)] + [whole()] * 7,
        out_specs=(whole(), whole(), whole()),
        scratch_shapes=[
            VMEM((keys.shape[0], 128), bf16),
            VMEM((n, rows, features + 128), bf16),
            VMEM((n, rows, features), bf16),
            VMEM((n, rows, 128), f32),
            VMEM((n, rows, features), bf16),
            VMEM((n, rows, 128), f32),
        ]
        + [dma((n,))] * 6
        + [dma((n_e,))] * 2
        + [dma((half, n_e))] * 4,
        compiler_params=pltpu.CompilerParams(
            collective_id=0, has_side_effects=True, vmem_limit_bytes=56 * 2**20
        ),
        name="attention_gather",
    )(queries, parent, leaf, routes, gate_weights, node, keys, values, residual)


def expert_kernel(
    n, n_e, k_steps, stream, gain, meta, w_gate, w_up, w_down, out,
    inverse, pick, mix, gate, up, hidden, outs, part, buf_s, acc, buf_c, zsend, buf_z, own,
    s_send, s_recv, c_send, c_recv, z_send, z_recv,
):
    f = pl.program_id(0)
    me, my_e = lax.axis_index("dp"), lax.axis_index("expert")
    rows, features = out.shape
    half = n // 2
    chip, core = me // 2, me % 2
    sibling = chip * 2 + (1 - core)
    tokens, width = stream.shape
    local, per, columns = outs.shape
    tile = w_gate.shape[1]
    base = my_e * local
    first_down = local * k_steps
    per_e = features // columns * local
    last = n_e * per_e - 1
    phase = f % k_steps

    def slot_keys(values, owner):
        return [
            (values[i].astype(jnp.int32) - base, owner * CAP + values[2 + i].astype(jnp.int32)) for i in range(2)
        ]

    @pl.when(f == 0)
    def _():
        wait_all = greet(
            [((chip + j) % half) * 2 + core for j in range(1, half)] + [sibling],
            [(my_e + k) % n_e for k in range(1, n_e)],
        )

        def square(i, carry):
            cut = pl.ds(pl.multiple_of(i * 64, 64), 64)
            wide = stream[cut, :].astype(jnp.float32)
            mean = jnp.mean(wide * wide, axis=1, keepdims=True)
            inverse[cut, :] = jnp.broadcast_to(lax.rsqrt(mean + EPS), (64, 128))
            return carry

        lax.fori_loop(0, tokens // 64, square, 0)
        info = meta[...].astype(jnp.float32)
        values = [info[:, META + i : META + i + 1] for i in range(6)]
        owner = lax.broadcasted_iota(jnp.int32, (tokens, 1), 0) // rows
        spot = lax.broadcasted_iota(jnp.int32, (tokens, local * per), 1)
        total = jnp.zeros((tokens, local * per), jnp.float32)
        for i, (expert, slot) in enumerate(slot_keys(values, owner)):
            target = jnp.where((expert >= 0) & (expert < local), expert * per + slot, -1)
            total = total + jnp.where(spot == target, values[4 + i], 0.0)
        mix[...] = total.astype(jnp.bfloat16)
        wait_all()

    @pl.when((f < first_down) & (phase == 0))
    def _():
        info = meta[...].astype(jnp.float32).T
        values = [info[META + i : META + i + 1, :] for i in range(4)]
        owner = lax.broadcasted_iota(jnp.int32, (1, tokens), 1) // rows
        spot = lax.broadcasted_iota(jnp.int32, (per, tokens), 0)
        x = f // k_steps
        hits = [spot == jnp.where(expert == x, slot, -1) for expert, slot in slot_keys(values, owner)]
        pick[...] = (hits[0] | hits[1]).astype(jnp.float32).astype(jnp.bfloat16)

    @pl.when(f < first_down)
    def _():
        cut = pl.ds(pl.multiple_of(phase * tile, tile), tile)
        wide = stream[:, cut].astype(jnp.float32)
        normed = (wide * inverse[:, 0:1] * gain[:, cut].astype(jnp.float32)).astype(jnp.bfloat16)
        data = jnp.dot(pick[...], normed, preferred_element_type=jnp.float32).astype(jnp.bfloat16)
        gate_term = jnp.dot(data, w_gate[0], preferred_element_type=jnp.float32)
        up_term = jnp.dot(data, w_up[0], preferred_element_type=jnp.float32)

        @pl.when(phase == 0)
        def _():
            gate[...] = gate_term
            up[...] = up_term

        @pl.when(phase > 0)
        def _():
            gate[...] += gate_term
            up[...] += up_term

    for x in range(local):
        @pl.when(f == (x + 1) * k_steps - 1)
        def _():
            value = gate[...]
            hidden[x] = (value / (1.0 + jnp.exp(-value)) * up[...]).astype(jnp.bfloat16)

    @pl.when(f >= first_down)
    def _():
        step = f - first_down
        x = step % local
        outs[x] = jnp.dot(hidden[x], w_down[0], preferred_element_type=jnp.float32).astype(jnp.bfloat16)

        @pl.when(x == local - 1)
        def _():
            cut = pl.ds(pl.multiple_of(step // local * columns, columns), columns)
            both = outs[...].reshape(local * per, columns)
            part[:, cut] = jnp.dot(mix[...], both, preferred_element_type=jnp.float32).astype(jnp.bfloat16)

    def spot(j, e, side):
        owner = ((chip + j) % half) * 2 + side
        return (pl.ds(pl.multiple_of(owner * rows, rows), rows), pl.ds(e * features, features))

    def s_copy(j, e):
        return remote(
            part.at[spot(j, e, 1 - core)], buf_s.at[j, e], s_send.at[j, e], s_recv.at[j, e], "dp", sibling
        )

    def c_copy(j, e):
        peer = ((chip + j) % half) * 2 + core
        return remote(acc.at[j, e], buf_c.at[j, e], c_send.at[j, e], c_recv.at[j, e], "dp", peer)

    def z_copy(e):
        return remote(zsend.at[e], buf_z.at[my_e], z_send.at[e], z_recv.at[my_e], "expert", e)

    def z_from(e):
        return remote(zsend.at[e], buf_z.at[e], z_send.at[e], z_recv.at[e], "expert", e)

    far = [j for j in range(1, half)] + [0]

    def to_core(e):
        for j in far:
            s_copy(j, e).start()

    def to_chips(e):
        for j in far:
            s_copy(j, e).wait_recv()
            total = part[spot(j, e, core)].astype(jnp.float32) + buf_s[j, e].astype(jnp.float32)
            acc[j, e] = total.astype(jnp.bfloat16)
            if j > 0:
                c_copy(j, e).start()

    def to_expert(e):
        total = acc[0, e].astype(jnp.float32)
        for j in range(1, half):
            c_copy(j, e).wait_recv()
            total = total + buf_c[j, e].astype(jnp.float32)

        @pl.when(my_e == e)
        def _():
            own[...] = total

        @pl.when(my_e != e)
        def _():
            zsend[e] = total.astype(jnp.bfloat16)
            z_copy(e).start()

    events = []
    for e in range(n_e):
        events.append(((e + 1) * per_e - 1, 0, to_core, e))
        events.append(((e + 1) * per_e, 1, to_chips, e))
        events.append(((e + 2) * per_e, 2, to_expert, e))
    events.sort(key=lambda event: (event[0], event[1], event[3]))
    for at, _, act, e in events:
        pl.when(f == first_down + min(at, last))(functools.partial(act, e))

    @pl.when(f == first_down + last)
    def _():
        for e in range(n_e):
            @pl.when(my_e != e)
            def _():
                z_from(e).wait_recv()
                own[...] += buf_z[e].astype(jnp.float32)

        mine = (
            pl.ds(pl.multiple_of(me * rows, rows), rows),
            pl.ds(pl.multiple_of(my_e * features, features), features),
        )
        out[...] = (stream[mine].astype(jnp.float32) + own[...]).astype(jnp.bfloat16)
        for e in range(n_e):
            for j in range(half):
                s_copy(j, e).wait_send()
                if j > 0:
                    c_copy(j, e).wait_send()

            @pl.when(my_e != e)
            def _():
                z_copy(e).wait_send()


def run_experts(stream, gain, meta, w_gate, w_up, w_down, n, n_e):
    tokens, width = stream.shape
    rows, features = tokens // n, width // n_e
    half = n // 2
    local, _, hidden = w_gate.shape
    per = n * CAP
    tile = 512
    k_steps = width // tile
    first_down = local * k_steps
    bf16, f32 = jnp.bfloat16, jnp.float32
    dma = pltpu.SemaphoreType.DMA
    fixed = lambda f: (0, 0)

    def wide(f):
        step = jnp.minimum(f, first_down - 1)
        return (step // k_steps, step % k_steps, 0)

    def tall(f):
        step = jnp.maximum(f - first_down, 0)
        return (step % local, 0, step // local)

    once = pl.Buffered(1)
    return pl.pallas_call(
        functools.partial(expert_kernel, n, n_e, k_steps),
        grid=(2 * first_down,),
        out_shape=jax.ShapeDtypeStruct((rows, features), bf16),
        in_specs=[
            pl.BlockSpec((tokens, width), fixed, pipeline_mode=once),
            pl.BlockSpec((1, width), fixed),
            pl.BlockSpec((tokens, 128), fixed),
            pl.BlockSpec((1, tile, hidden), wide),
            pl.BlockSpec((1, tile, hidden), wide),
            pl.BlockSpec((1, hidden, tile), tall),
        ],
        out_specs=pl.BlockSpec((rows, features), fixed),
        scratch_shapes=[
            VMEM((tokens, 128), f32),
            VMEM((per, tokens), bf16),
            VMEM((tokens, local * per), bf16),
            VMEM((per, hidden), f32),
            VMEM((per, hidden), f32),
            VMEM((local, per, hidden), bf16),
            VMEM((local, per, tile), bf16),
            VMEM((tokens, width), bf16),
            VMEM((half, n_e, rows, features), bf16),
            VMEM((half, n_e, rows, features), bf16),
            VMEM((half, n_e, rows, features), bf16),
            VMEM((n_e, rows, features), bf16),
            VMEM((n_e, rows, features), bf16),
            VMEM((rows, features), f32),
        ]
        + [dma((half, n_e))] * 4
        + [dma((n_e,))] * 2,
        compiler_params=pltpu.CompilerParams(
            dimension_semantics=("arbitrary",), collective_id=1, has_side_effects=True,
            vmem_limit_bytes=58 * 2**20,
        ),
        name="experts_scatter",
    )(stream, gain, meta, w_gate, w_up, w_down)


def body(
    residual, queries, cache_keys, cache_values, node_of_position, parent, leaf_ids, routes,
    gate_weights, norm_gain, w_gate, w_up, w_down,
):
    n, n_e = lax.axis_size("dp"), lax.axis_size("expert")
    rows = queries.shape[0]
    attention_out, stream, meta = attend_and_gather(
        queries, parent, leaf_ids.reshape(1, -1), routes.T, gate_weights.T, node_of_position.reshape(1, -1),
        cache_keys, cache_values, residual, n, n_e,
    )
    layer_out = run_experts(
        stream, norm_gain.reshape(1, -1), meta.reshape(n * rows, 128), w_gate, w_up, w_down, n, n_e
    )
    return attention_out, layer_out


def solution(mesh):
    in_specs = (
        P("dp", "expert"),
        P("dp", "expert"),
        P("dp", "expert"),
        P("dp", "expert"),
        P("dp"),
        P(),
        P("dp"),
        P("dp", None),
        P("dp", None),
        P(),
        P("expert", None, "dp"),
        P("expert", None, "dp"),
        P("expert", "dp", None),
    )
    out_specs = (P("dp", "expert"), P("dp", "expert"))
    return jax.shard_map(body, mesh=mesh, in_specs=in_specs, out_specs=out_specs, check_vma=False)
```
